32 devices in a mesh: section: 2 (over x), expert: 4 (over y, core), tensor: 4 (over z).
Axes of the slice: x: 2, y: 2, z: 4, core: 2. Of those that a mesh axis runs over, the one named last changes fastest.
Arguments:
- inputs: bfloat16 [2, 1024, 1024], P(None, 'expert'), may hold values from -6 to 6
- cotangent: bfloat16 [2, 1024, 1024], P(None, 'expert'), may hold values from -6 to 6
- seq_lengths: int32 [2, 16], P(None, 'expert'), may hold values from 0 to 256, as said below
- routes: int32 [2, 1024, 8], P(None, 'expert'), may hold values from 0 to 31, all different within a row; in each aligned block of 256 rows (0 to 255, 256 to 511, ..., all dimensions but the last counted through in order) at most 72 rows name the same one
- gain_attn: bfloat16 [2, 1024], P('section'), may hold values from 0.25 to 1.75
- w_query: bfloat16 [2, 1024, 1024], P('section', None, 'tensor'), may hold values from -0.1875 to 0.1875
- key_projection: bfloat16 [2, 1024, 512], P('section', None, 'tensor'), may hold values from -0.1875 to 0.1875
- value_projection: bfloat16 [2, 1024, 512], P('section', None, 'tensor'), may hold values from -0.1875 to 0.1875
- w_out: bfloat16 [2, 1024, 1024], P('section', 'tensor'), may hold values from -0.75 to 0.75
- gain_moe: bfloat16 [2, 1024], P('section'), may hold values from 0.25 to 1.75
- w_router: bfloat16 [2, 1024, 32], P('section'), may hold values from -0.09375 to 0.09375
- w_gate: bfloat16 [2, 32, 1024, 512], P('section', 'expert', None, 'tensor'), may hold values from -0.1875 to 0.1875
- w_up: bfloat16 [2, 32, 1024, 512], P('section', 'expert', None, 'tensor'), may hold values from -0.1875 to 0.1875
- w_down: bfloat16 [2, 32, 512, 1024], P('section', 'expert', 'tensor'), may hold values from -1 to 1
Outputs:
- activations: bfloat16 [2, 2, 1024, 1024], P('section', None, 'expert')
- input_grads: bfloat16 [2, 2, 1024, 1024], P('section', None, 'expert')
- grad_gain_attn: float32 [2, 1024], P('section')
- grad_query: float32 [2, 1024, 1024], P('section', None, 'tensor')
- grad_key: float32 [2, 1024, 512], P('section', None, 'tensor')
- grad_value: float32 [2, 1024, 512], P('section', None, 'tensor')
- grad_out: float32 [2, 1024, 1024], P('section', 'tensor')
- grad_gain_moe: float32 [2, 1024], P('section')
- grad_router: float32 [2, 1024, 32], P('section')
- grad_gate: float32 [2, 32, 1024, 512], P('section', 'expert', None, 'tensor')
- grad_up: float32 [2, 32, 1024, 512], P('section', 'expert', None, 'tensor')
- grad_down: float32 [2, 32, 512, 1024], P('section', 'expert', 'tensor')
The draws below stay inside these ranges and needn't reach their ends.
Inputs may be any that keep to these rules, and one draw needn't show every extreme that they name: `seq_lengths`: for each micro-batch and each index of the expert axis the 4 lengths sum to between 128 and 256; in every micro-batch one index holds a single sequence of all 256 rows and zeros in its other entries. `routes`: each row names 8 different experts. Within the rows of one index of the expert axis in one micro-batch no expert is named by more than 72 rows, and in some of these blocks one expert is named by exactly 72.
All inputs are finite; a program needn't handle non-finite values.
Results may differ from the reference program's by a relative error of at most 0.025.
Values may be sent and summed in bfloat16 or wider, within the bound.
No kernel may reach another device: no remote copies, remote signals or barrier semaphores. Data moves between devices by JAX's collectives and lax.ppermute only.
A program may use at most 256 MiB of HBM per device.

```python
import math
import jax
import jax.numpy as jnp
import numpy as np
from jax import lax

MODEL_WIDTH = 1024
QUERY_HEADS = 16
KEY_VALUE_HEADS = 8
HEAD_SIZE = 64
NE = 32
TOPK = 8
FE = 512
TOKEN_ROWS = 256
MB = 2
SLOTS = 4
LAYER_COUNT = 2
TOKENS = 1024
SEQ_SLOTS = 16
CAP = 72
N_EXPERT = 4
N_TENSOR = 4


def draw_seq_lengths(key, part):
    key = jax.random.fold_in(key, 7)
    rank_count = SEQ_SLOTS // SLOTS
    live_key, cut_key, pick_key = jax.random.split(key, 3)
    live_total = jax.random.randint(live_key, (MB, rank_count, 1), TOKEN_ROWS // 2, TOKEN_ROWS + 1)
    cut_points = jax.random.randint(cut_key, (MB, rank_count, SLOTS - 1), 0, TOKEN_ROWS + 1)
    cut_points = jnp.sort(cut_points * live_total // TOKEN_ROWS, axis=-1)
    edges = jnp.concatenate([jnp.zeros((MB, rank_count, 1), jnp.int32), cut_points, live_total], axis=-1)
    lengths = edges[:, :, 1:] - edges[:, :, :-1]
    full_rank = jax.random.randint(pick_key, (MB, 1), 0, rank_count)
    chosen_rank = (jnp.arange(rank_count, dtype=jnp.int32)[None, :] == full_rank)[:, :, None]
    whole_seq = jnp.where(jnp.arange(SLOTS, dtype=jnp.int32) == 0, TOKEN_ROWS, 0)[None, None, :]
    lengths = jnp.where(chosen_rank, whole_seq, lengths)
    return lengths.reshape(MB, SEQ_SLOTS).astype(jnp.int32)


def block_levels(rng, shape, shards, smallest, largest):
    level = 1.0
    for dim, blocks in shards:
        draws = jax.random.uniform(jax.random.fold_in(jax.random.fold_in(rng, 6), dim), (blocks,), jnp.float32, smallest / len(shards), largest / len(shards))
        level = level * jnp.repeat(jnp.exp(draws), shape[dim] // blocks).reshape((-1,) + (1,) * (len(shape) - 1 - dim))
    return level


def assign_block(own_key, own, number, rows, amount, top, limit, skew):
    ranking = jax.random.permutation(own_key, amount)
    crowded, usual = load_shares(amount, rows * top, limit, skew, True), load_shares(amount, rows * top, limit, skew, False)
    places = jnp.arange(amount)

    def named(tallies, rotation):
        used = int((tallies > 0).sum())
        fixed = max(1, used // 4)
        shifted = fixed + (places - fixed + rotation * (used - fixed)) % max(1, amount - fixed)
        return jnp.zeros((amount,), jnp.int32).at[ranking[jnp.where(places < fixed, places, shifted)]].set(jnp.asarray(tallies, jnp.int32))

    tallies = jnp.where(number % 4 == 0, named(crowded, number // 4), named(usual, number - number // 4 - 1))
    mixed = jax.random.permutation(jax.random.fold_in(own, 3), amount)
    giver, taker = mixed[0:amount // 2 * 2:2], mixed[1:amount // 2 * 2:2]
    room = jnp.minimum(tallies[giver] - 1, limit - tallies[taker]) // 2
    room = jnp.where((giver == ranking[0]) | (taker == ranking[0]) | (tallies[taker] == 0), 0, jnp.maximum(room, 0))
    shifted = jax.random.randint(jax.random.fold_in(own, 4), (amount // 2,), 0, 1 << 20) % (room + 1)
    tallies = tallies.at[giver].add(-shifted).at[taker].add(shifted)
    items = jnp.searchsorted(jnp.cumsum(tallies), jnp.arange(rows * top), side="right").astype(jnp.int32)
    table = items.reshape(top, rows).T
    table = table[jax.random.permutation(jax.random.fold_in(own, 1), rows)]
    rotation = jax.random.randint(jax.random.fold_in(own, 2), (rows, 1), 0, top)
    return jnp.take_along_axis(table, (jnp.arange(top)[None, :] + rotation) % top, axis=1)


def load_shares(number_of, total, reach, slope, full):
    loads = [(1 << 20) // math.isqrt(grade ** slope) + 1 for grade in range(1, number_of + 1)]
    largest = reach if full else min(reach, max(-(-total // number_of), total * loads[0] // sum(loads)))
    least = 1 if total - largest >= number_of - 1 else 0
    holding, rest = [largest] + [least] * (number_of - 1), total - largest - least * (number_of - 1)
    while rest > 0:
        free = [i for i in range(1, number_of) if holding[i] < largest] or [i for i in range(1, number_of) if holding[i] < reach]
        pool, left = sum([loads[i] for i in free]), rest
        for i in free:
            extra = min(reach - holding[i], max(1, left * loads[i] // pool), rest)
            holding[i] = holding[i] + extra
            rest = rest - extra
    return np.array(holding)


def scatter_about(stream_key, dims, deviation, reach, pieces=(), kind=jnp.bfloat16):
    gain = block_levels(stream_key, dims, pieces, -0.22, 0.18) if pieces else 1.0
    drawn = jax.random.normal(stream_key, dims, jnp.float32) * deviation * gain
    return jnp.minimum(jnp.maximum(drawn, -reach), reach).astype(kind)


def setup_inputs(seed: int = 0) -> dict:
    key_list = jax.random.split(jax.random.key(seed), 15)
    inputs = scatter_about(key_list[0], (MB, TOKENS, MODEL_WIDTH), 1.0, 6.0, ((1, 4),))
    cotangent = scatter_about(key_list[1], (MB, TOKENS, MODEL_WIDTH), 1.0, 6.0, ((1, 4),))
    seq_lengths = draw_seq_lengths(jax.random.fold_in(key_list[14], 71), 0)
    routes_keys = jax.random.split(jax.random.fold_in(key_list[3], 1), MB * TOKENS // TOKEN_ROWS)
    routes_turns = jax.random.permutation(jax.random.fold_in(key_list[3], 3), MB * TOKENS // TOKEN_ROWS)
    routes = jax.vmap(lambda own, number: assign_block(jax.random.fold_in(key_list[3], 2), own, number, TOKEN_ROWS, NE, TOPK, CAP, 1))(routes_keys, routes_turns).reshape((MB, TOKENS, TOPK))
    gain_attn = jnp.clip(1.0 + 0.15 * jax.random.normal(key_list[4], (LAYER_COUNT, MODEL_WIDTH), jnp.float32), 0.25, 1.75).astype(jnp.bfloat16)
    w_query = scatter_about(key_list[5], (LAYER_COUNT, MODEL_WIDTH, QUERY_HEADS * HEAD_SIZE), MODEL_WIDTH ** -0.5, 0.1875, ((0, 2), (2, 4)))
    key_projection = scatter_about(key_list[6], (LAYER_COUNT, MODEL_WIDTH, KEY_VALUE_HEADS * HEAD_SIZE), MODEL_WIDTH ** -0.5, 0.1875, ((0, 2), (2, 4)))
    value_projection = scatter_about(key_list[7], (LAYER_COUNT, MODEL_WIDTH, KEY_VALUE_HEADS * HEAD_SIZE), MODEL_WIDTH ** -0.5, 0.1875, ((0, 2), (2, 4)))
    w_out = scatter_about(key_list[8], (LAYER_COUNT, QUERY_HEADS * HEAD_SIZE, MODEL_WIDTH), (QUERY_HEADS * HEAD_SIZE // 16) ** -0.5, 0.75, ((0, 2), (1, 4)))
    gain_moe = jnp.clip(1.0 + 0.15 * jax.random.normal(key_list[9], (LAYER_COUNT, MODEL_WIDTH), jnp.float32), 0.25, 1.75).astype(jnp.bfloat16)
    w_router = scatter_about(key_list[10], (LAYER_COUNT, MODEL_WIDTH, NE), (4 * MODEL_WIDTH) ** -0.5, 0.09375, ((0, 2),))
    w_gate = scatter_about(key_list[11], (LAYER_COUNT, NE, MODEL_WIDTH, FE), MODEL_WIDTH ** -0.5, 0.1875, ((0, 2), (1, 4), (3, 4)))
    w_up = scatter_about(key_list[12], (LAYER_COUNT, NE, MODEL_WIDTH, FE), MODEL_WIDTH ** -0.5, 0.1875, ((0, 2), (1, 4), (3, 4)))
    w_down = scatter_about(key_list[13], (LAYER_COUNT, NE, FE, MODEL_WIDTH), (FE // 16) ** -0.5, 1.0, ((0, 2), (1, 4), (2, 4)))
    return dict(inputs=inputs, cotangent=cotangent, seq_lengths=seq_lengths, routes=routes, gain_attn=gain_attn, w_query=w_query, key_projection=key_projection, value_projection=value_projection, w_out=w_out, gain_moe=gain_moe, w_router=w_router, w_gate=w_gate, w_up=w_up, w_down=w_down)


EPSILON = 1e-06
THETA_BASE = 10000.0
MASKED = -1e+30
HIGHEST = lax.Precision.HIGHEST

@jax.custom_vjp
def lower_part(v):
    return lax.optimization_barrier(v.astype(jnp.bfloat16)).astype(jnp.float32)

@jax.custom_vjp
def lower_part_backward(v):
    return v

def low_keep(v):
    return (lower_part(v), None)

def low_pass(kept, grad):
    return (grad,)

def back_keep(v):
    return (v, None)

def back_low(kept, grad):
    return (lower_part(grad),)
lower_part.defvjp(low_keep, low_pass)
lower_part_backward.defvjp(back_keep, back_low)

def matrix_product(left, right):
    return jnp.dot(left, right, precision=HIGHEST)

def rms_scale(values):
    return lax.rsqrt(lax.optimization_barrier(jnp.mean(values * values, axis=-1, keepdims=True)) + EPSILON)

def layout(lengths, row_count, slot_count):
    row_ids = jnp.arange(row_count, dtype=jnp.int32)
    seq_ends = jnp.cumsum(lengths).astype(jnp.int32)
    starts = jnp.concatenate([seq_ends - lengths, seq_ends[-1:]]).astype(jnp.int32)
    segment = lax.optimization_barrier(jnp.sum((row_ids[:, None] >= seq_ends[None, :]).astype(jnp.int32), axis=1)).astype(jnp.int32)
    picked = segment[:, None] == jnp.arange(slot_count + 1, dtype=jnp.int32)[None, :]
    begins = lax.optimization_barrier(jnp.sum(jnp.where(picked, starts[None, :], 0), axis=1)).astype(jnp.int32)
    return (segment, (row_ids - begins).astype(jnp.float32))

def tables(position, head_dim):
    frequency = THETA_BASE ** (-jnp.arange(0, head_dim, 2, dtype=jnp.float32) / head_dim)
    angles = position[:, None] * frequency[None, :]
    cosine_lookup = jnp.concatenate([jnp.cos(angles), jnp.cos(angles)], axis=-1)[:, None, :]
    sine_lookup = jnp.concatenate([jnp.sin(angles), jnp.sin(angles)], axis=-1)[:, None, :]
    return (cosine_lookup, sine_lookup)

def rotary_apply(values, cosine_lookup, sine_lookup):
    half_dim = values.shape[-1] // 2
    turned = jnp.concatenate([-values[..., half_dim:], values[..., :half_dim]], axis=-1)
    return values * cosine_lookup + turned * sine_lookup

def slot_tables(route_ids, live_rows, expert_count, capacity):
    row_count, top_count = route_ids.shape
    flat_ids = route_ids.reshape(-1)
    keeping = jnp.repeat(live_rows, top_count)
    hits = ((flat_ids[:, None] == jnp.arange(expert_count, dtype=jnp.int32)[None, :]) & keeping[:, None]).astype(jnp.int32)
    before = (jnp.cumsum(hits, axis=0) - hits).astype(jnp.int32)
    place = lax.optimization_barrier(jnp.sum(before * hits, axis=1)).astype(jnp.int32)
    owner = jnp.where(keeping, flat_ids, expert_count).astype(jnp.int32)
    pair_count = row_count * top_count
    table = jnp.full((expert_count, capacity), pair_count, jnp.int32)
    table = table.at[owner, place].set(jnp.arange(pair_count, dtype=jnp.int32), mode='drop')
    return (owner, place, table)

def layer(resid, weights, route_ids, lengths):
    gain_a, w_q, key_weight, value_weight, w_o, gain_m, w_r, w_g, w_u, w_d = weights
    query_groups = QUERY_HEADS // KEY_VALUE_HEADS
    segment, position = layout(lengths, TOKEN_ROWS, SLOTS)
    live_rows = segment < SLOTS
    cosine_lookup, sine_lookup = tables(position, HEAD_SIZE)
    normalized_input = lower_part(resid * rms_scale(resid) * gain_a)
    query_matrix = rotary_apply(lower_part_backward(matrix_product(normalized_input, w_q)).reshape(TOKEN_ROWS, QUERY_HEADS, HEAD_SIZE), cosine_lookup, sine_lookup)
    query_matrix = lower_part(query_matrix).reshape(TOKEN_ROWS, KEY_VALUE_HEADS, query_groups, HEAD_SIZE)
    key_rows = lower_part(rotary_apply(lower_part_backward(matrix_product(normalized_input, key_weight)).reshape(TOKEN_ROWS, KEY_VALUE_HEADS, HEAD_SIZE), cosine_lookup, sine_lookup))
    value_rows = lower_part(lower_part_backward(matrix_product(normalized_input, value_weight))).reshape(TOKEN_ROWS, KEY_VALUE_HEADS, HEAD_SIZE)
    scores = lower_part_backward(jnp.einsum('qhgd,khd->hgqk', query_matrix, key_rows, precision=HIGHEST) * HEAD_SIZE ** (-0.5))
    row_ids = jnp.arange(TOKEN_ROWS, dtype=jnp.int32)
    allowed = (segment[:, None] == segment[None, :]) & (row_ids[None, :] <= row_ids[:, None])
    probs = jax.nn.softmax(jnp.where(allowed, scores, MASKED), axis=-1)
    mixed = jnp.einsum('hgqk,khd->qhgd', lower_part(probs), value_rows, precision=HIGHEST).reshape(TOKEN_ROWS, QUERY_HEADS * HEAD_SIZE)
    attended = lower_part(lower_part_backward(mixed))
    middle = resid + lower_part_backward(matrix_product(attended, w_o))
    normed_mid = lower_part(middle * rms_scale(middle) * gain_m)
    logits = lower_part_backward(matrix_product(normed_mid, w_r))
    chooser = route_ids[:, :, None] == jnp.arange(NE, dtype=jnp.int32)[None, None, :]
    chosen = lax.optimization_barrier(jnp.sum(jnp.where(chooser, logits[:, None, :], 0.0), axis=-1))
    gates = jax.nn.softmax(chosen, axis=-1) * live_rows[:, None]
    owner, place, table = slot_tables(route_ids, live_rows, NE, CAP)
    valid = table < TOKEN_ROWS * TOPK
    source = jnp.minimum(table // TOPK, TOKEN_ROWS - 1)
    dispatched = jnp.where(valid[:, :, None], normed_mid[source], 0.0)
    group_width = FE // N_TENSOR
    copies = lower_part_backward(jnp.broadcast_to(dispatched[None], (N_TENSOR, NE, CAP, MODEL_WIDTH)))
    gate_h = lower_part_backward(jnp.einsum('tecd,edtf->tecf', copies, w_g.reshape(NE, MODEL_WIDTH, N_TENSOR, group_width), precision=HIGHEST))
    up_h = lower_part_backward(jnp.einsum('tecd,edtf->tecf', copies, w_u.reshape(NE, MODEL_WIDTH, N_TENSOR, group_width), precision=HIGHEST))
    hidden = lower_part(jax.nn.silu(gate_h) * up_h)
    part = lower_part(lower_part_backward(jnp.einsum('tecf,etfd->tecd', hidden, w_d.reshape(NE, N_TENSOR, group_width, MODEL_WIDTH), precision=HIGHEST)))
    summed = lax.optimization_barrier(jnp.sum(part, axis=0)).reshape(NE * CAP, MODEL_WIDTH)
    slot_index = jnp.minimum(owner, NE - 1) * CAP + place
    picked = summed[slot_index].reshape(TOKEN_ROWS, TOPK, MODEL_WIDTH)
    moe = jnp.einsum('rk,rkd->rd', gates, picked, precision=HIGHEST)
    return lower_part_backward(lower_part(middle + moe))

def reference(inputs, cotangent, seq_lengths, routes, gain_attn, w_query, key_projection, value_projection, w_out, gain_moe, w_router, w_gate, w_up, w_down):
    block_count = MB * N_EXPERT
    first_in = inputs.astype(jnp.float32).reshape(block_count, TOKEN_ROWS, MODEL_WIDTH)
    lengths_all = seq_lengths.reshape(block_count, SLOTS)
    routes_all = routes.reshape(block_count, TOKEN_ROWS, TOPK)
    weights = tuple((member.astype(jnp.float32) for member in (gain_attn, w_query, key_projection, value_projection, w_out, gain_moe, w_router, w_gate, w_up, w_down)))

    def run_layer(layer_no, layer_inputs, params):
        chosen_params = tuple((member[layer_no] for member in params))

        def one_block(block_item):
            return layer(block_item[0], chosen_params, block_item[1], block_item[2])
        return lax.map(jax.checkpoint(one_block), (layer_inputs, routes_all, lengths_all))

    def forward(layer_inputs, params, between):
        first_out = run_layer(0, layer_inputs, params)
        second_out = run_layer(1, first_out + between, params)
        return (first_out, second_out)
    outputs, pullback = jax.vjp(forward, first_in, weights, jnp.zeros_like(first_in))
    grad_first, grad_weights, grad_between = pullback((jnp.zeros_like(outputs[0]), cotangent.astype(jnp.float32).reshape(block_count, TOKEN_ROWS, MODEL_WIDTH)))
    activations = jnp.stack([outputs[0], outputs[1]]).reshape(2, MB, TOKEN_ROWS * N_EXPERT, MODEL_WIDTH).astype(jnp.bfloat16)
    input_grads = jnp.stack([grad_first, grad_between]).reshape(2, MB, TOKEN_ROWS * N_EXPERT, MODEL_WIDTH).astype(jnp.bfloat16)
    return (activations, input_grads, grad_weights[0], grad_weights[1], grad_weights[2], grad_weights[3], grad_weights[4], grad_weights[5], grad_weights[6], grad_weights[7], grad_weights[8], grad_weights[9])
```

```python
import functools

import jax
import jax.numpy as jnp
from jax import lax
from jax.experimental import pallas as pl
from jax.experimental.pallas import tpu as pltpu
from jax.sharding import PartitionSpec as P

QUERY_HEADS = 16
KEY_VALUE_HEADS = 8
HEAD_SIZE = 64
NE = 32
SLOTS = 4
LANES = 128

EPSILON = 1e-06
THETA_BASE = 10000.0
MASKED = -1e30
TILE = 256
GROUPS = QUERY_HEADS // KEY_VALUE_HEADS
SCORE_SCALE = HEAD_SIZE ** (-0.5)
VMEM_LIMIT = 60 * 1024 * 1024

f32 = jnp.float32
bf16 = jnp.bfloat16


def dot_nn(a, b):
    return lax.dot_general(a, b, (((1,), (0,)), ((), ())), preferred_element_type=f32)


def dot_nt(a, b):
    return lax.dot_general(a, b, (((1,), (1,)), ((), ())), preferred_element_type=f32)


def dot_tn(a, b):
    return lax.dot_general(a, b, (((0,), (0,)), ((), ())), preferred_element_type=f32)


def swap(x, axis, k):
    return lax.ppermute(x, axis, [(i, i ^ k) for i in range(lax.axis_size(axis))])


def shifted(x, by):
    length = lax.axis_size("section")
    return lax.ppermute(x, "section", [(i, i + by) for i in range(length) if 0 <= i + by < length])


def expert_bits():
    n = lax.axis_size("expert")
    bits = []
    k = n // 2
    while k >= 1:
        bits.append(k)
        k //= 2
    return bits


def pieces_tensor(x):
    return [x] + [swap(x, "tensor", k) for k in range(1, lax.axis_size("tensor"))]


def gather_expert(x):
    for k in expert_bits():
        x = jnp.concatenate([x, swap(x, "expert", k)], axis=0)
    return x


def gather_rows(shard):
    low = jnp.concatenate(pieces_tensor(shard), axis=0)
    bits = expert_bits()
    for k in bits[:-1]:
        low = jnp.concatenate([low, swap(low, "expert", k)], axis=0)
    return (low, swap(low, "expert", bits[-1]))


def reduce_rows(low, high):
    bits = list(reversed(expert_bits()))
    for k in bits[:-1]:
        got = swap(high, "expert", k)
        half = low.shape[0] // 2
        high = (low[half:].astype(f32) + got[half:].astype(f32)).astype(bf16)
        low = (low[:half].astype(f32) + got[:half].astype(f32)).astype(bf16)
    got = swap(high, "expert", bits[-1])
    n = lax.axis_size("tensor")
    part = low.shape[0] // n
    cut = [slice(k * part, (k + 1) * part) for k in range(n)]
    total = low[cut[0]].astype(f32) + got[cut[0]].astype(f32)
    sent = [
        swap((low[cut[k]].astype(f32) + got[cut[k]].astype(f32)).astype(bf16), "tensor", k)
        for k in range(1, n)
    ]
    for piece in sent:
        total = total + piece.astype(f32)
    return total


def reduce_pieces(pieces):
    total = pieces[0].astype(f32)
    for k in range(1, len(pieces)):
        total = total + swap(pieces[k], "tensor", k).astype(f32)
    return total


def sum_expert(y):
    bits = list(reversed(expert_bits()))
    for k in bits:
        half = y.shape[0] // 2
        low = (lax.axis_index("expert") & k) == 0
        mine = jnp.where(low, y[:half], y[half:])
        other = jnp.where(low, y[half:], y[:half])
        y = (mine.astype(f32) + swap(other, "expert", k).astype(f32)).astype(y.dtype)
    for k in reversed(bits):
        low = (lax.axis_index("expert") & k) == 0
        theirs = swap(y, "expert", k)
        y = jnp.concatenate([jnp.where(low, y, theirs), jnp.where(low, theirs, y)], axis=0)
    return y


def sum_all_small(y):
    n = lax.axis_size("tensor")
    y = y + sum(swap(y, "tensor", k) for k in range(1, n))
    for k in expert_bits():
        y = y + swap(y, "expert", k)
    return y


def relative(x, axis, index, count):
    shape = x.shape
    k = count // 2
    while k >= 1:
        outer = count // (2 * k)
        inner = shape[axis] // (outer * 2)
        view = x.reshape(shape[:axis] + (outer, 2, inner) + shape[axis + 1 :])
        flipped = jnp.flip(view, axis=axis + 1)
        x = jnp.where((index & k) != 0, flipped, view).reshape(shape)
        k //= 2
    return x


def rope(v, cosine, sine):
    lane = lax.broadcasted_iota(jnp.int32, v.shape, 1) % HEAD_SIZE
    width = v.shape[1]
    left = pltpu.roll(v, width - HEAD_SIZE // 2, 1)
    right = pltpu.roll(v, HEAD_SIZE // 2, 1)
    return v * cosine + jnp.where(lane < HEAD_SIZE // 2, left, right) * sine


def rope_t(g, cosine, sine):
    return rope(g, cosine, -sine)


def twice(v, upper):
    lane = lax.broadcasted_iota(jnp.int32, v.shape, 1)
    keep = lane >= HEAD_SIZE if upper else lane < HEAD_SIZE
    return jnp.where(keep, v, pltpu.roll(v, HEAD_SIZE, 1))


def halves(v):
    lane = lax.broadcasted_iota(jnp.int32, v.shape, 1)
    return (jnp.where(lane < HEAD_SIZE, v, 0.0), jnp.where(lane >= HEAD_SIZE, v, 0.0))


def both(low, high):
    lane = lax.broadcasted_iota(jnp.int32, low.shape, 1)
    return jnp.where(lane < HEAD_SIZE, low, high)


def attn_forward_kernel(count, *refs):
    x_refs = refs[1 : 1 + count]
    gain_ref, wqkv_ref, wo_ref, cos_ref, sin_ref, mask_ref = refs[1 + count : 7 + count]
    part_refs = refs[7 + count : 7 + 2 * count]
    qkv_ref, mixed_ref, normed_ref = refs[7 + 2 * count :]
    x = jnp.concatenate([r[...] for r in x_refs], axis=0).astype(f32)
    scale = lax.rsqrt(jnp.mean(x * x, axis=-1, keepdims=True) + EPSILON)
    normed = (x * scale * gain_ref[...]).astype(bf16)
    normed_ref[...] = normed
    qkv = dot_nn(normed, wqkv_ref[...])
    cosine, sine = cos_ref[...], sin_ref[...]
    q_width = wo_ref.shape[0]
    kv_width = (qkv.shape[1] - q_width) // 2
    groups = []
    for at in range(0, qkv.shape[1], 128):
        piece = qkv[:, at : at + 128]
        if at < q_width + kv_width:
            piece = rope(piece, cosine, sine)
        piece = piece.astype(bf16)
        qkv_ref[:, at : at + 128] = piece
        groups.append(piece.astype(f32))
    allowed = mask_ref[...] > 0.0
    mixed = []
    for g in range(kv_width // HEAD_SIZE):
        k = twice(groups[q_width // 128 + g // 2], g % 2).astype(bf16)
        v = twice(groups[(q_width + kv_width) // 128 + g // 2], g % 2).astype(bf16)
        outs = []
        for q in halves(groups[g]):
            s = jnp.where(allowed, dot_nt(q.astype(bf16), k) * SCORE_SCALE, MASKED)
            p = jnp.exp(s - jnp.max(s, axis=-1, keepdims=True))
            p = (p / jnp.sum(p, axis=-1, keepdims=True)).astype(bf16)
            outs.append(dot_nn(p, v))
        mixed.append(both(*outs).astype(bf16))
    mixed = jnp.concatenate(mixed, axis=1)
    mixed_ref[...] = mixed
    part = dot_nn(mixed, wo_ref[...]).astype(bf16)
    rows = part.shape[0] // count
    for j in range(count):
        part_refs[j][...] = part[j * rows : (j + 1) * rows]


def attn_backward_kernel(count, *refs):
    gm_refs = refs[1 : 1 + count]
    x_refs = refs[1 + count : 1 + 2 * count]
    qkv_ref, wqkv_ref, wo_ref, cos_ref, sin_ref, mask_ref = refs[1 + 2 * count : 7 + 2 * count]
    part_refs = refs[7 + 2 * count : 7 + 3 * count]
    gqkv_ref, gain_ref, gm_ref = refs[7 + 3 * count :]
    gm = jnp.concatenate([r[...] for r in gm_refs], axis=0)
    gm_ref[...] = gm
    cosine, sine = cos_ref[...], sin_ref[...]
    q_width = wo_ref.shape[0]
    kv_width = (qkv_ref.shape[1] - q_width) // 2
    gmix = dot_nt(gm, wo_ref[...]).astype(bf16).astype(f32)
    allowed = mask_ref[...] > 0.0
    grads = [None] * (qkv_ref.shape[1] // 128)
    for g in range(kv_width // HEAD_SIZE):
        k_at = q_width // 128 + g // 2
        v_at = (q_width + kv_width) // 128 + g // 2
        k = twice(qkv_ref[:, k_at * 128 : k_at * 128 + 128].astype(f32), g % 2).astype(bf16)
        v = twice(qkv_ref[:, v_at * 128 : v_at * 128 + 128].astype(f32), g % 2).astype(bf16)
        qs = halves(qkv_ref[:, g * 128 : g * 128 + 128].astype(f32))
        gxs = halves(gmix[:, g * 128 : g * 128 + 128])
        gqs, gk, gv = [], None, None
        for q, gx in zip(qs, gxs):
            q, gx = q.astype(bf16), gx.astype(bf16)
            s = jnp.where(allowed, dot_nt(q, k) * SCORE_SCALE, MASKED)
            p = jnp.exp(s - jnp.max(s, axis=-1, keepdims=True))
            p = p / jnp.sum(p, axis=-1, keepdims=True)
            gp = dot_nt(gx, v)
            gs = p * (gp - jnp.sum(p * gp, axis=-1, keepdims=True))
            gqs.append(dot_nn(gs.astype(bf16), k) * SCORE_SCALE)
            gk_h = dot_nn(gs.T.astype(bf16), q)
            gv_h = dot_nn(p.T.astype(bf16), gx)
            gk = gk_h if gk is None else gk + gk_h
            gv = gv_h if gv is None else gv + gv_h
        grads[g] = both(*gqs)
        gk = (gk + pltpu.roll(gk, HEAD_SIZE, 1)) * SCORE_SCALE
        gv = gv + pltpu.roll(gv, HEAD_SIZE, 1)
        grads[k_at] = gk if g % 2 == 0 else both(grads[k_at], gk)
        grads[v_at] = gv if g % 2 == 0 else both(grads[v_at], gv)
    for j in range(len(grads)):
        piece = grads[j]
        if j * 128 < q_width + kv_width:
            piece = rope_t(piece, cosine, sine)
        grads[j] = piece.astype(bf16)
    gqkv = jnp.concatenate(grads, axis=1)
    gqkv_ref[...] = gqkv
    part = dot_nt(gqkv, wqkv_ref[...])
    rows = part.shape[0] // count
    for j in range(count):
        part_refs[j][...] = part[j * rows : (j + 1) * rows].astype(bf16)
    x = jnp.concatenate([r[...] for r in x_refs], axis=0).astype(f32)
    scale = lax.rsqrt(jnp.mean(x * x, axis=-1, keepdims=True) + EPSILON)
    gain_ref[...] = jnp.sum(part * x * scale, axis=0, keepdims=True)


def pick_half(low_ref, high_ref, steps):
    return jnp.where(pl.program_id(0) < steps // 2, high_ref[...], low_ref[...])


def put_half(low_ref, high_ref, steps, value):
    @pl.when(pl.program_id(0) < steps // 2)
    def _():
        high_ref[...] = value

    @pl.when(pl.program_id(0) >= steps // 2)
    def _():
        low_ref[...] = value


def expert_forward_kernel(
    steps, dep_ref, xl_ref, xh_ref, sel_ref, wr_ref, wcat_ref, wd_ref, low_ref, high_ref, probs_ref
):
    x = pick_half(xl_ref, xh_ref, steps)
    sel = sel_ref[...]
    width = wd_ref.shape[0]
    count = width // 128
    logits = jnp.where(sel > 0.0, dot_nn(x, wr_ref[...]), MASKED)
    probs = jnp.exp(logits - jnp.max(logits, axis=-1, keepdims=True)) * sel
    probs = probs / jnp.maximum(jnp.sum(probs, axis=-1, keepdims=True), 1e-30)
    probs_ref[...] = probs
    hidden = []
    for e in range(count):
        h = dot_nn(x, wcat_ref[:, e * 256 : (e + 1) * 256])
        gate, up = h[:, :128], h[:, 128:]
        hidden.append((gate * jax.nn.sigmoid(gate) * up * probs[:, e : e + 1]).astype(bf16))
    out = dot_nn(jnp.concatenate(hidden, axis=1), wd_ref[...]).astype(bf16)
    put_half(low_ref, high_ref, steps, out)


def expert_backward_kernel(
    steps, dep_ref, xl_ref, xh_ref, gl_ref, gh_ref, sel_ref, wr_ref, wcat_ref, wd_ref,
    low_ref, high_ref, act_ref, hid_ref, glog_ref,
):
    x = pick_half(xl_ref, xh_ref, steps)
    gy = pick_half(gl_ref, gh_ref, steps)
    sel = sel_ref[...]
    width = wd_ref.shape[0]
    count = width // 128
    logits = jnp.where(sel > 0.0, dot_nn(x, wr_ref[...]), MASKED)
    probs = jnp.exp(logits - jnp.max(logits, axis=-1, keepdims=True)) * sel
    probs = probs / jnp.maximum(jnp.sum(probs, axis=-1, keepdims=True), 1e-30)
    lane = lax.broadcasted_iota(jnp.int32, probs.shape, 1)
    grad_act = dot_nt(gy, wd_ref[...])
    grad_gates = jnp.zeros(probs.shape, f32)
    pieces = []
    for e in range(count):
        h = dot_nn(x, wcat_ref[:, e * 256 : (e + 1) * 256])
        gate, up = h[:, :128], h[:, 128:]
        s = jax.nn.sigmoid(gate)
        silu = gate * s
        hid = silu * up
        ga = grad_act[:, e * 128 : (e + 1) * 128]
        p = probs[:, e : e + 1]
        grad_gates = jnp.where(
            lane == e, jnp.sum(hid * ga, axis=-1, keepdims=True), grad_gates
        )
        gp = ga * p
        pieces.append((gp * up * s * (1.0 + gate * (1.0 - s))).astype(bf16))
        pieces.append((gp * silu).astype(bf16))
        hid_ref[:, e * 128 : (e + 1) * 128] = (hid * p).astype(bf16)
    gcat = jnp.concatenate(pieces, axis=1)
    act_ref[...] = gcat
    glog = probs * (grad_gates - jnp.sum(probs * grad_gates, axis=-1, keepdims=True))
    glog = glog.astype(bf16)
    glog_ref[...] = glog
    out = (dot_nt(gcat, wcat_ref[...]) + dot_nt(glog, wr_ref[...])).astype(bf16)
    put_half(low_ref, high_ref, steps, out)


def expert_weights_kernel(count, micro_count, *refs):
    xt_refs = refs[1 : 1 + count]
    gy_refs = refs[1 + count : 1 + 2 * count]
    act_refs = refs[1 + 2 * count : 1 + 2 * count + micro_count]
    hid_refs = refs[1 + 2 * count + micro_count : 1 + 2 * count + 2 * micro_count]
    gate_ref, up_ref, down_ref = refs[1 + 2 * count + 2 * micro_count :]
    rows = gy_refs[0].shape[0]
    per = count // micro_count
    for at in range(0, xt_refs[0].shape[0], 256):
        grads = sum(
            dot_nn(
                xt_refs[j][at : at + 256, :],
                act_refs[j // per][(j % per) * rows : (j % per + 1) * rows, :],
            )
            for j in range(count)
        )
        for j in range(grads.shape[1] // 256):
            gate_ref[j, at : at + 256, :] = grads[:, j * 256 : j * 256 + 128]
            up_ref[j, at : at + 256, :] = grads[:, j * 256 + 128 : j * 256 + 256]
    down = sum(
        dot_nn(hid_refs[j // per][:, (j % per) * rows : (j % per + 1) * rows], gy_refs[j][...])
        for j in range(count)
    )
    for j in range(down.shape[0] // 128):
        down_ref[j] = down[j * 128 : (j + 1) * 128, :]


def full(array):
    zeros = (0,) * array.ndim
    return pl.BlockSpec(array.shape, lambda *_: zeros)


def once(array):
    zeros = (0,) * array.ndim
    return pl.BlockSpec(array.shape, lambda *_: zeros, pipeline_mode=pl.Buffered(1))


ANYWHERE = pl.BlockSpec(memory_space=pl.ANY)


def params():
    return pltpu.CompilerParams(vmem_limit_bytes=VMEM_LIMIT)


def cost(flops, moved):
    return pl.CostEstimate(flops=int(flops), bytes_accessed=int(moved), transcendentals=0)


def attn_forward(dep, xs, gain, wqkv, wo, cosine, sine, mask):
    count = len(xs)
    part, width = xs[0].shape
    rows = part * count
    heads = wqkv.shape[1]
    args = (*xs, gain, wqkv, wo, cosine, sine, mask)
    outs = (jax.ShapeDtypeStruct((part, width), bf16),) * count + (
        jax.ShapeDtypeStruct((rows, heads), bf16),
        jax.ShapeDtypeStruct((rows, wo.shape[0]), bf16),
        jax.ShapeDtypeStruct((rows, width), bf16),
    )
    out = pl.pallas_call(
        functools.partial(attn_forward_kernel, count),
        out_shape=outs,
        in_specs=[ANYWHERE] + [full(a) for a in args],
        out_specs=[full(o) for o in outs],
        compiler_params=params(),
        cost_estimate=cost(2 * rows * width * (heads + wo.shape[0]), 4e6),
        name="attn_forward",
    )(dep, *args)
    return (out[:count], *out[count:])


def attn_backward(dep, gms, xs, qkv, wqkv, wo, cosine, sine, mask):
    count = len(xs)
    part, width = xs[0].shape
    rows = part * count
    heads = wqkv.shape[1]
    args = (*gms, *xs, qkv, wqkv, wo, cosine, sine, mask)
    outs = (jax.ShapeDtypeStruct((part, width), bf16),) * count + (
        jax.ShapeDtypeStruct((rows, heads), bf16),
        jax.ShapeDtypeStruct((1, width), f32),
        jax.ShapeDtypeStruct((rows, width), bf16),
    )
    out = pl.pallas_call(
        functools.partial(attn_backward_kernel, count),
        out_shape=outs,
        in_specs=[ANYWHERE] + [full(a) for a in args],
        out_specs=[full(o) for o in outs],
        compiler_params=params(),
        cost_estimate=cost(2 * rows * width * (heads + wo.shape[0]), 4e6),
        name="attn_backward",
    )(dep, *args)
    return (out[:count], *out[count:])


def half_specs(rows, width):
    half = rows // (2 * TILE)
    low = pl.BlockSpec((TILE, width), lambda i: (jnp.maximum(i - half, 0), 0))
    high = pl.BlockSpec((TILE, width), lambda i: (jnp.minimum(i, half - 1), 0))
    whole = lambda w: pl.BlockSpec((TILE, w), lambda i: ((i + half) % (2 * half), 0))
    return (low, high, whole)


def expert_forward(dep, x, sel, wr, wcat, wd):
    half, width = x[0].shape
    rows = 2 * half
    low, high, whole = half_specs(rows, width)
    outs = (
        jax.ShapeDtypeStruct((half, width), bf16),
        jax.ShapeDtypeStruct((half, width), bf16),
        jax.ShapeDtypeStruct((rows, LANES), f32),
    )
    return pl.pallas_call(
        functools.partial(expert_forward_kernel, rows // TILE),
        out_shape=outs,
        grid=(rows // TILE,),
        in_specs=[ANYWHERE, low, high, whole(LANES), once(wr), once(wcat), once(wd)],
        out_specs=[low, high, whole(LANES)],
        compiler_params=params(),
        cost_estimate=cost(2 * rows * 3 * wcat.size / 2, 12e6),
        name="expert_forward",
    )(dep, *x, sel, wr, wcat, wd)


def expert_backward(dep, x, gy, sel, wr, wcat, wd):
    half, width = x[0].shape
    rows = 2 * half
    low, high, whole = half_specs(rows, width)
    outs = (
        jax.ShapeDtypeStruct((half, width), bf16),
        jax.ShapeDtypeStruct((half, width), bf16),
        jax.ShapeDtypeStruct((rows, wcat.shape[1]), bf16),
        jax.ShapeDtypeStruct((rows, wd.shape[0]), bf16),
        jax.ShapeDtypeStruct((rows, LANES), bf16),
    )
    return pl.pallas_call(
        functools.partial(expert_backward_kernel, rows // TILE),
        out_shape=outs,
        grid=(rows // TILE,),
        in_specs=[ANYWHERE, low, high, low, high, whole(LANES), once(wr), once(wcat), once(wd)],
        out_specs=[low, high, whole(wcat.shape[1]), whole(wd.shape[0]), whole(LANES)],
        compiler_params=params(),
        cost_estimate=cost(2 * rows * 5 * wcat.size / 2, 20e6),
        name="expert_backward",
    )(dep, *x, *gy, sel, wr, wcat, wd)


def expert_weights(dep, xts, gys, acts, hids):
    micro_count = len(acts)
    count = len(xts)
    width, half = xts[0].shape
    rows = acts[0].shape[0]
    local = hids[0].shape[0] // 128
    pair = 2 if rows <= 1024 else 1
    outs = (
        jax.ShapeDtypeStruct((local, width, 128), f32),
        jax.ShapeDtypeStruct((local, width, 128), f32),
        jax.ShapeDtypeStruct((local, 128, width), f32),
    )
    return pl.pallas_call(
        functools.partial(expert_weights_kernel, count, micro_count),
        out_shape=outs,
        grid=(local // pair,),
        in_specs=[ANYWHERE]
        + [once(a) for a in xts]
        + [once(a) for a in gys]
        + [pl.BlockSpec((rows, 256 * pair), lambda i: (0, i))] * micro_count
        + [pl.BlockSpec((128 * pair, rows), lambda i: (i, 0))] * micro_count,
        out_specs=[
            pl.BlockSpec((pair, width, 128), lambda i: (i, 0, 0)),
            pl.BlockSpec((pair, width, 128), lambda i: (i, 0, 0)),
            pl.BlockSpec((pair, 128, width), lambda i: (i, 0, 0)),
        ],
        compiler_params=params(),
        cost_estimate=cost(2 * micro_count * rows * width * 3 * 128 * local, 36e6),
        name="expert_weights",
    )(dep, *xts, *gys, *acts, *hids)


def rms_scale(values):
    return lax.rsqrt(jnp.mean(values * values, axis=-1, keepdims=True) + EPSILON)


def norm_backward(grad_normed, values, scale_rows, gain):
    weighted = grad_normed * gain
    return scale_rows * weighted - values * scale_rows**3 * jnp.mean(
        values * weighted, axis=-1, keepdims=True
    )


def layout(lengths, row_ids):
    seq_ends = jnp.cumsum(lengths)
    starts = jnp.concatenate([seq_ends - lengths, seq_ends[-1:]])
    segment = jnp.sum((row_ids[:, None] >= seq_ends[None, :]).astype(jnp.int32), axis=1)
    picked = segment[:, None] == jnp.arange(SLOTS + 1, dtype=jnp.int32)[None, :]
    begins = jnp.sum(jnp.where(picked, starts[None, :], 0), axis=1)
    return (segment, (row_ids - begins).astype(f32))


def tables(position):
    frequency = THETA_BASE ** (-jnp.arange(0, HEAD_SIZE, 2, dtype=f32) / HEAD_SIZE)
    angles = position[:, None] * frequency[None, :]
    cosine, sine = jnp.cos(angles), jnp.sin(angles)
    cosine = jnp.concatenate([cosine] * 4, axis=-1)
    sine = jnp.concatenate([-sine, sine] * 2, axis=-1)
    return (cosine, sine)


def local(
    inputs,
    cotangent,
    seq_lengths,
    routes,
    gain_attn,
    w_query,
    key_projection,
    value_projection,
    w_out,
    gain_moe,
    w_router,
    w_gate,
    w_up,
    w_down,
):
    first = lax.axis_index("section") == 0
    e_no = lax.axis_index("expert")
    t_no = lax.axis_index("tensor")
    n_t = lax.axis_size("tensor")
    micro_count, rows, width = inputs.shape
    local_experts = w_gate.shape[1]
    micro = range(micro_count)
    part = rows // n_t

    gain_a = gain_attn.astype(f32)
    gain_m = gain_moe.astype(f32)
    wqkv = jnp.concatenate([w_query[0], key_projection[0], value_projection[0]], axis=1)
    wo = w_out[0]
    wr = jnp.pad(jnp.roll(w_router[0], -e_no * local_experts, axis=1), ((0, 0), (0, LANES - NE)))
    wcat = jnp.concatenate(
        [jnp.swapaxes(w_gate[0], 0, 1), jnp.swapaxes(w_up[0], 0, 1)], axis=2
    ).reshape(width, 256 * local_experts)
    wd = w_down[0].reshape(local_experts * 128, width)

    base = jnp.arange(rows, dtype=jnp.int32)
    row_ids = (((base // part) ^ t_no) * part) + base % part
    x_rel = relative(inputs, 1, t_no, n_t)
    routes_rel = relative(routes, 1, t_no, n_t)
    cosines, sines, masks, sels = [], [], [], []
    for m in micro:
        segment, position = layout(seq_lengths[m], row_ids)
        cosine, sine = tables(position)
        cosines.append(cosine)
        sines.append(sine)
        allowed = (segment[:, None] == segment[None, :]) & (row_ids[None, :] <= row_ids[:, None])
        masks.append(allowed.astype(f32))
        named = jnp.where((segment < SLOTS)[:, None], routes_rel[m], -1)
        sels.append(gather_expert(named))
    for m in micro:
        named = sels[m]
        shift = (jnp.arange(NE, dtype=jnp.int32) + e_no * local_experts) % NE
        shift = jnp.where(jnp.arange(LANES) < NE, jnp.pad(shift, (0, LANES - NE)), -2)
        sels[m] = jnp.any(named[:, :, None] == shift[None, None, :], axis=1).astype(f32)

    def attend(m, dep, xs):
        parts, qkv, mixed, normed = attn_forward(
            dep, xs, gain_a, wqkv, wo, cosines[m], sines[m], masks[m]
        )
        middle = xs[0].astype(f32) + reduce_pieces(parts)
        scale_mid = rms_scale(middle)
        normed_mid = (middle * scale_mid * gain_m).astype(bf16)
        return dict(
            xs=xs, qkv=qkv, mixed=mixed, normed=normed, middle=middle, scale_mid=scale_mid,
            rows=gather_rows(normed_mid),
        )

    def finish(saved, out):
        return (saved["middle"] + reduce_rows(out[0], out[1])).astype(bf16)

    def experts(m, dep, saved):
        return expert_forward(dep, saved["rows"], sels[m], wr, wcat, wd)

    def experts_back(m, dep, saved, gathered):
        return expert_backward(dep, saved["rows"], gathered, sels[m], wr, wcat, wd)

    def attend_back(m, dep, saved, grad_y, out):
        grad_normed = reduce_rows(out[0], out[1])
        middle, scale_mid = saved["middle"], saved["scale_mid"]
        g_gain_m = jnp.sum(grad_normed * middle * scale_mid, axis=0, keepdims=True)
        grad_middle = norm_backward(grad_normed, middle, scale_mid, gain_m) + grad_y.astype(f32)
        gms = pieces_tensor(grad_middle.astype(bf16))
        parts, gqkv, g_gain_a, gm = attn_backward(
            dep, gms, saved["xs"], saved["qkv"], wqkv, wo, cosines[m], sines[m], masks[m]
        )
        grad_normed_in = reduce_pieces(parts)
        resid = saved["xs"][0].astype(f32)
        grad_in = norm_backward(grad_normed_in, resid, rms_scale(resid), gain_a) + grad_middle
        return dict(
            gm=gm, gqkv=gqkv, g_gain_m=g_gain_m, g_gain_a=g_gain_a, grad_in=grad_in.astype(bf16)
        )

    def shared_grads(saved, outs, back):
        def total(left, right):
            return sum(dot_tn(saved[m][left], back[m][right]) for m in micro)

        g_router = sum(
            dot_tn(saved[m]["rows"][j], outs[m][4][j * half : (j + 1) * half])
            for m in micro
            for j in range(2)
        )
        return (
            total("normed", "gqkv"),
            total("mixed", "gm"),
            sum(back[m]["g_gain_a"] for m in micro),
            sum(back[m]["g_gain_m"] for m in micro),
            g_router,
        )

    def expert_grads(dep, saved, gathered, outs):
        return expert_weights(
            dep,
            [x.T for s in saved for x in s["rows"]],
            [g for pair in gathered for g in pair],
            [o[2] for o in outs],
            [o[3].T for o in outs],
        )

    half = rows * lax.axis_size("expert") // 2
    x_cut = [[x_rel[m, k * part : (k + 1) * part] for k in range(n_t)] for m in micro]
    cot = [relative(cotangent[m], 0, t_no, n_t)[:part] for m in micro]
    dep = wqkv

    saved0 = []
    for m in micro:
        saved0.append(attend(m, dep, x_cut[m]))
        dep = saved0[m]["qkv"]
    out0 = []
    for m in micro:
        out0.append(experts(m, dep, saved0[m]))
        dep = out0[m][2]
    shard0 = [finish(saved0[m], out0[m]) for m in micro]
    saved1 = []
    for m in micro:
        saved1.append(attend(m, dep, pieces_tensor(shifted(shard0[m], 1))))
        dep = saved1[m]["qkv"]
    gathered1 = [gather_rows(cot[m]) for m in micro]
    back_out1 = []
    for m in micro:
        back_out1.append(experts_back(m, dep, saved1[m], gathered1[m]))
        dep = back_out1[m][4]
    back1 = []
    for m in micro:
        back1.append(attend_back(m, dep, saved1[m], cot[m], back_out1[m]))
        dep = back1[m]["g_gain_a"]
    returned = [shifted(back1[m]["grad_in"], -1) for m in micro]
    experts1 = expert_grads(dep, saved1, gathered1, back_out1)
    dep = experts1[0]
    out1 = [experts(0, dep, saved1[0])]
    dep = out1[0][2]
    gathered0 = [gather_rows(returned[m]) for m in micro]
    back_out0 = []
    for m in micro:
        back_out0.append(experts_back(m, dep, saved0[m], gathered0[m]))
        dep = back_out0[m][4]
    for m in micro[1:]:
        out1.append(experts(m, dep, saved1[m]))
        dep = out1[m][2]
    shard1 = [finish(saved1[m], out1[m]) for m in micro]
    back0 = []
    for m in micro:
        back0.append(attend_back(m, dep, saved0[m], returned[m], back_out0[m]))
        dep = back0[m]["g_gain_a"]
    grads1 = shared_grads(saved1, back_out1, back1)
    grads0 = shared_grads(saved0, back_out0, back0)
    g_gate, g_up, g_down = lax.cond(
        first,
        lambda: tuple(expert_grads(dep, saved0, gathered0, back_out0)),
        lambda: tuple(experts1),
    )

    g_qkv, g_out, g_gain_a, g_gain_m, g_router = (
        jnp.where(first, a, b) for a, b in zip(grads0, grads1)
    )
    g_qkv = sum_expert(g_qkv.astype(bf16)).astype(f32)
    g_out = sum_expert(g_out.astype(bf16)).astype(f32)
    g_gains = sum_all_small(jnp.concatenate([g_gain_a, g_gain_m], axis=0))
    g_router = jnp.roll(g_router[:, :NE], e_no * local_experts, axis=1)
    g_router = lax.psum(g_router, ("expert", "tensor"))

    def assemble(shards):
        whole = [jnp.concatenate(pieces_tensor(s), axis=0) for s in shards]
        return jnp.stack([relative(w, 0, t_no, n_t) for w in whole])[None]

    activations = assemble([jnp.where(first, shard0[m], shard1[m]) for m in micro])
    input_grads = assemble(
        [jnp.where(first, back0[m]["grad_in"], back1[m]["grad_in"]) for m in micro]
    )
    q_width = w_query.shape[2]
    kv_width = key_projection.shape[2]
    return (
        activations,
        input_grads,
        g_gains[:1],
        g_qkv[None, :, :q_width],
        g_qkv[None, :, q_width : q_width + kv_width],
        g_qkv[None, :, q_width + kv_width :],
        g_out[None],
        g_gains[1:],
        g_router[None],
        g_gate[None],
        g_up[None],
        g_down[None],
    )


def solution(mesh):
    in_specs = (
        P(None, "expert", None),
        P(None, "expert", None),
        P(None, "expert"),
        P(None, "expert", None),
        P("section", None),
        P("section", None, "tensor"),
        P("section", None, "tensor"),
        P("section", None, "tensor"),
        P("section", "tensor", None),
        P("section", None),
        P("section", None, None),
        P("section", "expert", None, "tensor"),
        P("section", "expert", None, "tensor"),
        P("section", "expert", "tensor", None),
    )
    out_specs = (
        P("section", None, "expert", None),
        P("section", None, "expert", None),
        P("section", None),
        P("section", None, "tensor"),
        P("section", None, "tensor"),
        P("section", None, "tensor"),
        P("section", "tensor", None),
        P("section", None),
        P("section", None, None),
        P("section", "expert", None, "tensor"),
        P("section", "expert", None, "tensor"),
        P("section", "expert", "tensor", None),
    )
    return jax.shard_map(local, mesh=mesh, in_specs=in_specs, out_specs=out_specs, check_vma=False)
```

```python
import functools

import jax
import jax.numpy as jnp
from jax import lax
from jax.experimental import pallas as pl
from jax.experimental.pallas import tpu as pltpu
from jax.sharding import PartitionSpec as P

QUERY_HEADS = 16
KEY_VALUE_HEADS = 8
HEAD_SIZE = 64
NE = 32
SLOTS = 4
LANES = 128

EPSILON = 1e-06
THETA_BASE = 10000.0
MASKED = -1e30
TILE = 256
GROUPS = QUERY_HEADS // KEY_VALUE_HEADS
SCORE_SCALE = HEAD_SIZE ** (-0.5)
VMEM_LIMIT = 60 * 1024 * 1024

f32 = jnp.float32
bf16 = jnp.bfloat16


def dot_nn(a, b):
    return lax.dot_general(a, b, (((1,), (0,)), ((), ())), preferred_element_type=f32)


def dot_nt(a, b):
    return lax.dot_general(a, b, (((1,), (1,)), ((), ())), preferred_element_type=f32)


def dot_tn(a, b):
    return lax.dot_general(a, b, (((0,), (0,)), ((), ())), preferred_element_type=f32)


def swap(x, axis, k):
    return lax.ppermute(x, axis, [(i, i ^ k) for i in range(lax.axis_size(axis))])


def shifted(x, by):
    length = lax.axis_size("section")
    return lax.ppermute(x, "section", [(i, i + by) for i in range(length) if 0 <= i + by < length])


def expert_bits():
    n = lax.axis_size("expert")
    bits = []
    k = n // 2
    while k >= 1:
        bits.append(k)
        k //= 2
    return bits


def pieces_tensor(x):
    return [x] + [swap(x, "tensor", k) for k in range(1, lax.axis_size("tensor"))]


def after(value, *others):
    return lax.optimization_barrier((value, *others))[0]


def gather_far(own):
    blocks = [own]
    for k in expert_bits()[:-1]:
        blocks = blocks + [swap(block, "expert", k) for block in blocks]
    return blocks


def pair(block):
    return (block, swap(block, "expert", 1))


def gather_pairs(own):
    return [pair(block) for block in gather_far(own)]


def added(terms):
    return sum(term.astype(f32) for term in terms).astype(bf16)


def reduce_pairs(pairs):
    bits = expert_bits()
    terms = [[block, swap(other, "expert", bits[-1])] for block, other in pairs]
    sent = terms[0][0]
    for k in reversed(bits[:-1]):
        half = len(terms) // 2
        for j in range(half):
            sent = added(terms[half + j])
            terms[j].append(swap(sent, "expert", k))
        terms = terms[:half]
    return terms[0], sent


def reduce_pieces(pieces, *done):
    got = [swap(pieces[k], "tensor", k) for k in range(1, len(pieces))]
    if done:
        got[-1] = after(got[-1], *done)
    return sum((g.astype(f32) for g in got), pieces[0].astype(f32))


def gather_weight(w):
    low = (lax.axis_index("expert") & 1) == 0
    half = w.shape[0] // 2
    mine = jnp.where(low, w[:half], w[half:])
    far = jnp.concatenate(pieces_tensor(mine)[1:], axis=0)
    near = swap(far, "expert", 1)
    out = [w]
    for k in range(lax.axis_size("tensor") - 1):
        cut = slice(k * half, (k + 1) * half)
        out.append(jnp.where(low, far[cut], near[cut]))
        out.append(jnp.where(low, near[cut], far[cut]))
    return jnp.concatenate(out, axis=0)


def sum_expert(y):
    bits = list(reversed(expert_bits()))
    for k in bits:
        half = y.shape[0] // 2
        low = (lax.axis_index("expert") & k) == 0
        mine = jnp.where(low, y[:half], y[half:])
        other = jnp.where(low, y[half:], y[:half])
        y = (mine.astype(f32) + swap(other, "expert", k).astype(f32)).astype(y.dtype)
    for k in reversed(bits):
        low = (lax.axis_index("expert") & k) == 0
        theirs = swap(y, "expert", k)
        y = jnp.concatenate([jnp.where(low, y, theirs), jnp.where(low, theirs, y)], axis=0)
    return y


def sum_all_small(y):
    n = lax.axis_size("tensor")
    y = y + sum(swap(y, "tensor", k) for k in range(1, n))
    for k in expert_bits():
        y = y + swap(y, "expert", k)
    return y


def relative(x, axis, index, count):
    shape = x.shape
    k = count // 2
    while k >= 1:
        outer = count // (2 * k)
        inner = shape[axis] // (outer * 2)
        view = x.reshape(shape[:axis] + (outer, 2, inner) + shape[axis + 1 :])
        flipped = jnp.flip(view, axis=axis + 1)
        x = jnp.where((index & k) != 0, flipped, view).reshape(shape)
        k //= 2
    return x


def rope(v, cosine, sine):
    lane = lax.broadcasted_iota(jnp.int32, v.shape, 1) % HEAD_SIZE
    width = v.shape[1]
    left = pltpu.roll(v, width - HEAD_SIZE // 2, 1)
    right = pltpu.roll(v, HEAD_SIZE // 2, 1)
    return v * cosine + jnp.where(lane < HEAD_SIZE // 2, left, right) * sine


def rope_t(g, cosine, sine):
    return rope(g, cosine, -sine)


def twice(v, upper):
    lane = lax.broadcasted_iota(jnp.int32, v.shape, 1)
    keep = lane >= HEAD_SIZE if upper else lane < HEAD_SIZE
    return jnp.where(keep, v, pltpu.roll(v, HEAD_SIZE, 1))


def halves(v):
    lane = lax.broadcasted_iota(jnp.int32, v.shape, 1)
    return (jnp.where(lane < HEAD_SIZE, v, 0.0), jnp.where(lane >= HEAD_SIZE, v, 0.0))


def both(low, high):
    lane = lax.broadcasted_iota(jnp.int32, low.shape, 1)
    return jnp.where(lane < HEAD_SIZE, low, high)


def attn_forward_kernel(count, *refs):
    x_refs = refs[1 : 1 + count]
    gain_ref, wqkv_ref, cos_ref, sin_ref, mask_ref = refs[1 + count : 6 + count]
    mixed_ref, qkv_ref, normed_ref = refs[6 + count :]
    x = jnp.concatenate([r[...] for r in x_refs], axis=0).astype(f32)
    scale = lax.rsqrt(jnp.mean(x * x, axis=-1, keepdims=True) + EPSILON)
    normed = (x * scale * gain_ref[...]).astype(bf16)
    normed_ref[...] = normed
    qkv = dot_nn(normed, wqkv_ref[...])
    cosine, sine = cos_ref[0], sin_ref[0]
    q_width = mixed_ref.shape[1]
    kv_width = (qkv.shape[1] - q_width) // 2
    groups = []
    for at in range(0, qkv.shape[1], 128):
        piece = qkv[:, at : at + 128]
        if at < q_width + kv_width:
            piece = rope(piece, cosine, sine)
        piece = piece.astype(bf16)
        qkv_ref[:, at : at + 128] = piece
        groups.append(piece.astype(f32))
    allowed = mask_ref[0] > 0.0
    mixed = []
    for g in range(kv_width // HEAD_SIZE):
        k = twice(groups[q_width // 128 + g // 2], g % 2).astype(bf16)
        v = twice(groups[(q_width + kv_width) // 128 + g // 2], g % 2).astype(bf16)
        outs = []
        for q in halves(groups[g]):
            s = jnp.where(allowed, dot_nt(q.astype(bf16), k) * SCORE_SCALE, MASKED)
            p = jnp.exp(s - jnp.max(s, axis=-1, keepdims=True))
            p = (p / jnp.sum(p, axis=-1, keepdims=True)).astype(bf16)
            outs.append(dot_nn(p, v))
        mixed.append(both(*outs).astype(bf16))
    mixed_ref[...] = jnp.concatenate(mixed, axis=1)


def attn_project_kernel(count, *refs):
    mixed_refs = refs[1 : 1 + count]
    x_refs = refs[1 + count : 1 + 2 * count]
    wo_ref, gain_ref, rows_ref, middle_ref = refs[1 + 2 * count :]
    part = x_refs[0].shape[0]
    mixed = jnp.concatenate(
        [
            jnp.concatenate([r[(i ^ k) * part : ((i ^ k) + 1) * part, :] for i in range(count)], axis=0)
            for k, r in enumerate(mixed_refs)
        ],
        axis=1,
    )
    x = jnp.concatenate([r[...] for r in x_refs], axis=0).astype(f32)
    middle = x + dot_nn(mixed, wo_ref[...])
    scale = lax.rsqrt(jnp.mean(middle * middle, axis=-1, keepdims=True) + EPSILON)
    rows_ref[...] = (middle * scale * gain_ref[...]).astype(bf16)
    middle_ref[...] = middle[: middle_ref.shape[0]]


def split_kernel(terms, *refs):
    total = sum(r[...].astype(f32) for r in refs[1 : 1 + terms]).astype(bf16)
    outs = refs[1 + terms :]
    rows = total.shape[0] // len(outs)
    for j, out in enumerate(outs):
        out[...] = total[j * rows : (j + 1) * rows]


def attn_backward_kernel(count, *refs):
    gm_refs = refs[1 : 1 + count]
    x_refs = refs[1 + count : 1 + 2 * count]
    qkv_ref, wqkv_ref, wo_ref, cos_ref, sin_ref, mask_ref = refs[1 + 2 * count : 7 + 2 * count]
    part_refs = refs[7 + 2 * count : 7 + 3 * count]
    gqkv_ref, gain_ref, gm_ref = refs[7 + 3 * count :]
    gm = jnp.concatenate([r[...] for r in gm_refs], axis=0)
    gm_ref[...] = gm
    cosine, sine = cos_ref[0], sin_ref[0]
    q_width = wo_ref.shape[0]
    kv_width = (qkv_ref.shape[1] - q_width) // 2
    gmix = dot_nt(gm, wo_ref[...]).astype(bf16).astype(f32)
    allowed = mask_ref[0] > 0.0
    grads = [None] * (qkv_ref.shape[1] // 128)
    for g in range(kv_width // HEAD_SIZE):
        k_at = q_width // 128 + g // 2
        v_at = (q_width + kv_width) // 128 + g // 2
        k = twice(qkv_ref[:, k_at * 128 : k_at * 128 + 128].astype(f32), g % 2).astype(bf16)
        v = twice(qkv_ref[:, v_at * 128 : v_at * 128 + 128].astype(f32), g % 2).astype(bf16)
        qs = halves(qkv_ref[:, g * 128 : g * 128 + 128].astype(f32))
        gxs = halves(gmix[:, g * 128 : g * 128 + 128])
        gqs, gk, gv = [], None, None
        for q, gx in zip(qs, gxs):
            q, gx = q.astype(bf16), gx.astype(bf16)
            s = jnp.where(allowed, dot_nt(q, k) * SCORE_SCALE, MASKED)
            p = jnp.exp(s - jnp.max(s, axis=-1, keepdims=True))
            p = p / jnp.sum(p, axis=-1, keepdims=True)
            gp = dot_nt(gx, v)
            gs = p * (gp - jnp.sum(p * gp, axis=-1, keepdims=True))
            gqs.append(dot_nn(gs.astype(bf16), k) * SCORE_SCALE)
            gk_h = dot_nn(gs.T.astype(bf16), q)
            gv_h = dot_nn(p.T.astype(bf16), gx)
            gk = gk_h if gk is None else gk + gk_h
            gv = gv_h if gv is None else gv + gv_h
        grads[g] = both(*gqs)
        gk = (gk + pltpu.roll(gk, HEAD_SIZE, 1)) * SCORE_SCALE
        gv = gv + pltpu.roll(gv, HEAD_SIZE, 1)
        grads[k_at] = gk if g % 2 == 0 else both(grads[k_at], gk)
        grads[v_at] = gv if g % 2 == 0 else both(grads[v_at], gv)
    for j in range(len(grads)):
        piece = grads[j]
        if j * 128 < q_width + kv_width:
            piece = rope_t(piece, cosine, sine)
        grads[j] = piece.astype(bf16)
    gqkv = jnp.concatenate(grads, axis=1)
    gqkv_ref[...] = gqkv
    part = dot_nt(gqkv, wqkv_ref[...])
    rows = part.shape[0] // count
    for j in range(count):
        part_refs[j][...] = part[j * rows : (j + 1) * rows].astype(bf16)
    x = jnp.concatenate([r[...] for r in x_refs], axis=0).astype(f32)
    scale = lax.rsqrt(jnp.mean(x * x, axis=-1, keepdims=True) + EPSILON)
    gain_ref[0] = jnp.sum(part * x * scale, axis=0, keepdims=True)


def pick(first_ref, second_ref, steps):
    return jnp.where(pl.program_id(0) < steps // 2, first_ref[...], second_ref[...])


def put(first_ref, second_ref, steps, value):
    @pl.when(pl.program_id(0) < steps // 2)
    def _():
        first_ref[...] = value

    @pl.when(pl.program_id(0) >= steps // 2)
    def _():
        second_ref[...] = value


def expert_forward_kernel(
    steps, dep_ref, xa_ref, xb_ref, sa_ref, sb_ref, wr_ref, wg_ref, wu_ref, wd_ref,
    oa_ref, ob_ref,
):
    x = pick(xa_ref, xb_ref, steps)
    sel = pick(sa_ref, sb_ref, steps)
    width = wd_ref.shape[0]
    count = width // 128
    logits = jnp.where(sel > 0.0, dot_nn(x, wr_ref[...]), MASKED)
    probs = jnp.exp(logits - jnp.max(logits, axis=-1, keepdims=True)) * sel
    probs = probs / jnp.maximum(jnp.sum(probs, axis=-1, keepdims=True), 1e-30)
    hidden = []
    for e in range(count):
        h = dot_nn(x, jnp.concatenate([wg_ref[e], wu_ref[e]], axis=1))
        gate, up = h[:, :128], h[:, 128:]
        hidden.append((gate * jax.nn.sigmoid(gate) * up * probs[:, e : e + 1]).astype(bf16))
    out = dot_nn(jnp.concatenate(hidden, axis=1), wd_ref[...]).astype(bf16)
    put(oa_ref, ob_ref, steps, out)


def expert_backward_kernel(
    steps, dep_ref, xa_ref, xb_ref, ga_ref, gb_ref, sa_ref, sb_ref, wr_ref, wg_ref, wu_ref, wd_ref,
    oa_ref, ob_ref, act_ref, hid_ref, xt_ref, glog_ref,
):
    x = pick(xa_ref, xb_ref, steps)
    gy = pick(ga_ref, gb_ref, steps)
    sel = pick(sa_ref, sb_ref, steps)
    xt_ref[...] = x.astype(f32).T.astype(bf16)
    width = wd_ref.shape[0]
    count = width // 128
    logits = jnp.where(sel > 0.0, dot_nn(x, wr_ref[...]), MASKED)
    probs = jnp.exp(logits - jnp.max(logits, axis=-1, keepdims=True)) * sel
    probs = probs / jnp.maximum(jnp.sum(probs, axis=-1, keepdims=True), 1e-30)
    lane = lax.broadcasted_iota(jnp.int32, probs.shape, 1)
    grad_act = dot_nt(gy, wd_ref[...])
    grad_gates = jnp.zeros(probs.shape, f32)
    pieces = []
    for e in range(count):
        h = dot_nn(x, jnp.concatenate([wg_ref[e], wu_ref[e]], axis=1))
        gate, up = h[:, :128], h[:, 128:]
        s = jax.nn.sigmoid(gate)
        silu = gate * s
        hid = silu * up
        ga = grad_act[:, e * 128 : (e + 1) * 128]
        p = probs[:, e : e + 1]
        grad_gates = jnp.where(
            lane == e, jnp.sum(hid * ga, axis=-1, keepdims=True), grad_gates
        )
        gp = ga * p
        pieces.append((gp * up * s * (1.0 + gate * (1.0 - s))).astype(bf16))
        pieces.append((gp * silu).astype(bf16))
        hid_ref[e * 128 : (e + 1) * 128, :] = (hid * p).T.astype(bf16)
    gcat = jnp.concatenate(pieces, axis=1)
    act_ref[...] = gcat
    glog = probs * (grad_gates - jnp.sum(probs * grad_gates, axis=-1, keepdims=True))
    glog = glog.astype(bf16)
    glog_ref[...] = glog
    wcat = jnp.concatenate([w[e] for e in range(count) for w in (wg_ref, wu_ref)], axis=1)
    out = (dot_nt(gcat, wcat) + dot_nt(glog, wr_ref[...])).astype(bf16)
    put(oa_ref, ob_ref, steps, out)


def expert_weights_kernel(pairs, *refs):
    xt_refs = refs[1 : 1 + pairs]
    gy_refs = refs[1 + pairs : 1 + 3 * pairs]
    act_refs = refs[1 + 3 * pairs : 1 + 4 * pairs]
    hid_refs = refs[1 + 4 * pairs : 1 + 5 * pairs]
    glog_refs = refs[1 + 5 * pairs : 1 + 6 * pairs]
    gate_ref, up_ref, down_ref, router_ref = refs[1 + 6 * pairs :]
    rows = gy_refs[0].shape[0]

    @pl.when(pl.program_id(0) == 0)
    def _():
        for at in range(0, xt_refs[0].shape[0], 256):
            router_ref[at : at + 256, :] = sum(
                dot_nn(xt_refs[j][at : at + 256, :], glog_refs[j][...]) for j in range(pairs)
            )

    for at in range(0, xt_refs[0].shape[0], 256):
        grads = sum(dot_nn(xt_refs[j][at : at + 256, :], act_refs[j][...]) for j in range(pairs))
        for j in range(grads.shape[1] // 256):
            gate_ref[j, at : at + 256, :] = grads[:, j * 256 : j * 256 + 128]
            up_ref[j, at : at + 256, :] = grads[:, j * 256 + 128 : j * 256 + 256]
    down = sum(
        dot_nn(hid_refs[j // 2][:, (j % 2) * rows : (j % 2 + 1) * rows], gy_refs[j][...])
        for j in range(2 * pairs)
    )
    for j in range(down.shape[0] // 128):
        down_ref[j] = down[j * 128 : (j + 1) * 128, :]


def full(array):
    zeros = (0,) * array.ndim
    return pl.BlockSpec(array.shape, lambda *_: zeros)


def once(array):
    zeros = (0,) * array.ndim
    return pl.BlockSpec(array.shape, lambda *_: zeros, pipeline_mode=pl.Buffered(1))


ANYWHERE = pl.BlockSpec(memory_space=pl.ANY)


def params():
    return pltpu.CompilerParams(vmem_limit_bytes=VMEM_LIMIT)


def cost(flops, moved):
    return pl.CostEstimate(flops=int(flops), bytes_accessed=int(moved), transcendentals=0)


def by_micro(array, micro_count):
    if array.ndim == 3:
        return pl.BlockSpec((1,) + array.shape[1:], lambda m: (m, 0, 0))
    return pl.BlockSpec((array.shape[0] // micro_count, array.shape[1]), lambda m: (m, 0))


def attn_forward(dep, xs, gain, wqkv, q_width, cosine, sine, mask):
    count = len(xs)
    micro_count = mask.shape[0]
    width = xs[0].shape[1]
    rows = xs[0].shape[0] * count
    heads = wqkv.shape[1]
    split = lambda array: by_micro(array, micro_count)
    outs = (
        jax.ShapeDtypeStruct((rows, q_width), bf16),
        jax.ShapeDtypeStruct((rows, heads), bf16),
        jax.ShapeDtypeStruct((rows, width), bf16),
    )
    return pl.pallas_call(
        functools.partial(attn_forward_kernel, count),
        out_shape=outs,
        grid=(micro_count,),
        in_specs=[ANYWHERE]
        + [split(x) for x in xs]
        + [full(gain), full(wqkv), split(cosine), split(sine), split(mask)],
        out_specs=[split(o) for o in outs],
        compiler_params=params(),
        cost_estimate=cost(2 * rows * width * heads, 6e6),
        name="attn_forward",
    )(dep, *xs, gain, wqkv, cosine, sine, mask)


def attn_project(dep, mixed, xs, wo, gain, micro_count):
    count = len(xs)
    width = xs[0].shape[1]
    rows = xs[0].shape[0] * count
    split = lambda array: by_micro(array, micro_count)
    outs = (
        jax.ShapeDtypeStruct((rows, width), bf16),
        jax.ShapeDtypeStruct((rows // count, width), f32),
    )
    return pl.pallas_call(
        functools.partial(attn_project_kernel, count),
        out_shape=outs,
        grid=(micro_count,),
        in_specs=[ANYWHERE]
        + [split(x) for x in mixed]
        + [split(x) for x in xs]
        + [full(wo), full(gain)],
        out_specs=[split(o) for o in outs],
        compiler_params=params(),
        cost_estimate=cost(2 * rows * width * width, 6e6),
        name="attn_project",
    )(dep, *mixed, *xs, wo, gain)


def split_sum(dep, terms, count, micro_count):
    rows, width = terms[0].shape
    split = lambda array: by_micro(array, micro_count)
    outs = (jax.ShapeDtypeStruct((rows // count, width), bf16),) * count
    return pl.pallas_call(
        functools.partial(split_kernel, len(terms)),
        out_shape=outs,
        grid=(micro_count,),
        in_specs=[ANYWHERE] + [split(x) for x in terms],
        out_specs=[split(o) for o in outs],
        compiler_params=params(),
        cost_estimate=cost(rows * width * 4, 4e6),
        name="split_sum",
    )(dep, *terms)


def attn_backward(dep, gms, xs, qkv, wqkv, wo, cosine, sine, mask):
    count = len(xs)
    micro_count = mask.shape[0]
    part, width = xs[0].shape
    rows = part * count
    heads = wqkv.shape[1]
    split = lambda array: by_micro(array, micro_count)
    outs = (jax.ShapeDtypeStruct((part, width), bf16),) * count + (
        jax.ShapeDtypeStruct((rows, heads), bf16),
        jax.ShapeDtypeStruct((micro_count, 1, width), f32),
        jax.ShapeDtypeStruct((rows, width), bf16),
    )
    out = pl.pallas_call(
        functools.partial(attn_backward_kernel, count),
        out_shape=outs,
        grid=(micro_count,),
        in_specs=[ANYWHERE]
        + [split(x) for x in gms]
        + [split(x) for x in xs]
        + [split(qkv), full(wqkv), full(wo), split(cosine), split(sine), split(mask)],
        out_specs=[split(o) for o in outs],
        compiler_params=params(),
        cost_estimate=cost(2 * rows * width * (heads + wo.shape[0]), 8e6),
        name="attn_backward",
    )(dep, *gms, *xs, qkv, wqkv, wo, cosine, sine, mask)
    return (out[:count], *out[count:])


def pair_specs(rows):
    half = rows // TILE
    first = lambda w: pl.BlockSpec((TILE, w), lambda i: (jnp.minimum(i, half - 1), 0))
    second = lambda w: pl.BlockSpec((TILE, w), lambda i: (jnp.maximum(i - half, 0), 0))
    whole = lambda w: pl.BlockSpec((TILE, w), lambda i: (i, 0))
    return (first, second, whole)


def expert_forward(dep, x, sel, wr, wg, wu, wd):
    rows, width = x[0].shape
    steps = 2 * rows // TILE
    first, second, whole = pair_specs(rows)
    outs = (jax.ShapeDtypeStruct((rows, width), bf16),) * 2
    return pl.pallas_call(
        functools.partial(expert_forward_kernel, steps),
        out_shape=outs,
        grid=(steps,),
        in_specs=[ANYWHERE, first(width), second(width), first(LANES), second(LANES)]
        + [once(wr), once(wg), once(wu), once(wd)],
        out_specs=[first(width), second(width)],
        compiler_params=params(),
        cost_estimate=cost(4 * rows * 3 * wg.size, 12e6),
        name="expert_forward",
    )(dep, *x, *sel, wr, wg, wu, wd)


def expert_backward(dep, x, gy, sel, wr, wg, wu, wd):
    rows, width = x[0].shape
    steps = 2 * rows // TILE
    first, second, whole = pair_specs(rows)
    across = lambda h: pl.BlockSpec((h, TILE), lambda i: (0, i))
    outs = (
        jax.ShapeDtypeStruct((rows, width), bf16),
        jax.ShapeDtypeStruct((rows, width), bf16),
        jax.ShapeDtypeStruct((2 * rows, 2 * wd.shape[0]), bf16),
        jax.ShapeDtypeStruct((wd.shape[0], 2 * rows), bf16),
        jax.ShapeDtypeStruct((width, 2 * rows), bf16),
        jax.ShapeDtypeStruct((2 * rows, LANES), bf16),
    )
    return pl.pallas_call(
        functools.partial(expert_backward_kernel, steps),
        out_shape=outs,
        grid=(steps,),
        in_specs=[ANYWHERE, first(width), second(width), first(width), second(width)]
        + [first(LANES), second(LANES), once(wr), once(wg), once(wu), once(wd)],
        out_specs=[first(width), second(width), whole(2 * wd.shape[0])]
        + [across(wd.shape[0]), across(width), whole(LANES)],
        compiler_params=params(),
        cost_estimate=cost(4 * rows * 5 * wg.size, 20e6),
        name="expert_backward",
    )(dep, *x, *gy, *sel, wr, wg, wu, wd)


def expert_weights(dep, xts, gys, acts, hids, glogs):
    pairs = len(xts)
    width = xts[0].shape[0]
    rows = acts[0].shape[0]
    local = hids[0].shape[0] // 128
    pair = 2 if pairs * rows <= 2048 else 1
    outs = (
        jax.ShapeDtypeStruct((local, width, 128), f32),
        jax.ShapeDtypeStruct((local, width, 128), f32),
        jax.ShapeDtypeStruct((local, 128, width), f32),
        jax.ShapeDtypeStruct((width, LANES), f32),
    )
    return pl.pallas_call(
        functools.partial(expert_weights_kernel, pairs),
        out_shape=outs,
        grid=(local // pair,),
        in_specs=[ANYWHERE]
        + [once(a) for a in xts]
        + [once(a) for a in gys]
        + [pl.BlockSpec((rows, 256 * pair), lambda i: (0, i))] * pairs
        + [pl.BlockSpec((128 * pair, rows), lambda i: (i, 0))] * pairs
        + [once(a) for a in glogs],
        out_specs=[
            pl.BlockSpec((pair, width, 128), lambda i: (i, 0, 0)),
            pl.BlockSpec((pair, width, 128), lambda i: (i, 0, 0)),
            pl.BlockSpec((pair, 128, width), lambda i: (i, 0, 0)),
            full(outs[3]),
        ],
        compiler_params=params(),
        cost_estimate=cost(2 * pairs * rows * width * 3 * 128 * local, 36e6),
        name="expert_weights",
    )(dep, *xts, *gys, *acts, *hids, *glogs)


def rms_scale(values):
    return lax.rsqrt(jnp.mean(values * values, axis=-1, keepdims=True) + EPSILON)


def norm_backward(grad_normed, values, scale_rows, gain):
    weighted = grad_normed * gain
    return scale_rows * weighted - values * scale_rows**3 * jnp.mean(
        values * weighted, axis=-1, keepdims=True
    )


def layout(lengths, row_ids):
    seq_ends = jnp.cumsum(lengths)
    starts = jnp.concatenate([seq_ends - lengths, seq_ends[-1:]])
    segment = jnp.sum((row_ids[:, None] >= seq_ends[None, :]).astype(jnp.int32), axis=1)
    picked = segment[:, None] == jnp.arange(SLOTS + 1, dtype=jnp.int32)[None, :]
    begins = jnp.sum(jnp.where(picked, starts[None, :], 0), axis=1)
    return (segment, (row_ids - begins).astype(f32))


def tables(position):
    frequency = THETA_BASE ** (-jnp.arange(0, HEAD_SIZE, 2, dtype=f32) / HEAD_SIZE)
    angles = position[:, None] * frequency[None, :]
    cosine, sine = jnp.cos(angles), jnp.sin(angles)
    cosine = jnp.concatenate([cosine] * 4, axis=-1)
    sine = jnp.concatenate([-sine, sine] * 2, axis=-1)
    return (cosine, sine)


def local(
    inputs,
    cotangent,
    seq_lengths,
    routes,
    gain_attn,
    w_query,
    key_projection,
    value_projection,
    w_out,
    gain_moe,
    w_router,
    w_gate,
    w_up,
    w_down,
):
    first = lax.axis_index("section") == 0
    e_no = lax.axis_index("expert")
    t_no = lax.axis_index("tensor")
    n_t = lax.axis_size("tensor")
    micro_count, rows, width = inputs.shape
    local_experts = w_gate.shape[1]
    micro = range(micro_count)
    part = rows // n_t

    gain_a = gain_attn.astype(f32)
    gain_m = gain_moe.astype(f32)
    wqkv = jnp.concatenate([w_query[0], key_projection[0], value_projection[0]], axis=1)
    wo = w_out[0]
    wr = jnp.pad(jnp.roll(w_router[0], -e_no * local_experts, axis=1), ((0, 0), (0, LANES - NE)))
    wg, wu = w_gate[0], w_up[0]
    wd = w_down[0].reshape(local_experts * 128, width)

    base = jnp.arange(rows, dtype=jnp.int32)
    row_ids = (((base // part) ^ t_no) * part) + base % part
    q_width = w_query.shape[2]

    def cut(array):
        blocks = array.reshape(micro_count, n_t, part, array.shape[2])
        return [
            lax.dynamic_index_in_dim(blocks, t_no ^ k, 1, keepdims=False).reshape(
                micro_count * part, array.shape[2]
            )
            for k in range(n_t)
        ]

    def joined(pieces):
        whole = jnp.stack([p.reshape(micro_count, part, p.shape[1]) for p in pieces], axis=1)
        return whole.reshape(micro_count * rows, pieces[0].shape[1])

    x_cut = cut(inputs)
    cot = cut(cotangent)[0]
    cosines, sines, masks, lives = [], [], [], []
    for m in micro:
        segment, position = layout(seq_lengths[m], row_ids)
        cosine, sine = tables(position)
        cosines.append(cosine)
        sines.append(sine)
        allowed = (segment[:, None] == segment[None, :]) & (row_ids[None, :] <= row_ids[:, None])
        masks.append(allowed.astype(f32))
        lives.append(segment < SLOTS)
    cosine, sine, mask = jnp.stack(cosines), jnp.stack(sines), jnp.stack(masks)
    named = jnp.where(jnp.concatenate(lives)[:, None], joined(cut(routes)), -1)
    shift = (jnp.arange(NE, dtype=jnp.int32) + e_no * local_experts) % NE
    shift = jnp.where(jnp.arange(LANES) < NE, jnp.pad(shift, (0, LANES - NE)), -2)

    def selected(block):
        return jnp.any(block[:, :, None] == shift[None, None, :], axis=1).astype(f32)

    wo_all = gather_weight(wo)

    def attend(dep, xs, wo_all):
        mixed, qkv, normed = attn_forward(dep, xs, gain_a, wqkv, q_width, cosine, sine, mask)
        block, middle = attn_project(
            qkv, pieces_tensor(mixed), xs, wo_all, gain_m, micro_count
        )
        return dict(xs=xs, qkv=qkv, mixed=mixed, normed=normed, middle=middle, block=block)

    def finish(saved, pieces, *done):
        return (saved["middle"] + reduce_pieces(pieces, *done)).astype(bf16)

    def experts(dep, j, saved):
        return expert_forward(dep, saved["rows"][j], sels[j], wr, wg, wu, wd)

    def experts_back(dep, j, saved, gathered):
        return expert_backward(dep, saved["rows"][j], gathered[j], sels[j], wr, wg, wu, wd)

    def mid_back(saved, grad_y, pieces, done):
        grad_normed = reduce_pieces(pieces, done)
        middle = saved["middle"]
        scale_mid = rms_scale(middle)
        g_gain_m = jnp.sum(grad_normed * middle * scale_mid, axis=0, keepdims=True)
        grad_middle = norm_backward(grad_normed, middle, scale_mid, gain_m) + grad_y.astype(f32)
        return (g_gain_m, grad_middle)

    def attend_back(dep, saved, grad_middle, gm_shard):
        parts, gqkv, g_gain_a, gm = attn_backward(
            dep, pieces_tensor(gm_shard), saved["xs"], saved["qkv"], wqkv, wo, cosine, sine, mask
        )
        grad_normed_in = reduce_pieces(parts)
        resid = saved["xs"][0].astype(f32)
        grad_in = norm_backward(grad_normed_in, resid, rms_scale(resid), gain_a) + grad_middle
        return (gqkv, jnp.sum(g_gain_a, axis=0), gm, grad_in.astype(bf16))

    def shared_grads(saved, gqkv, gm):
        return (dot_tn(saved["normed"], gqkv), dot_tn(saved["mixed"], gm))

    def expert_grads(dep, gathered, outs):
        return expert_weights(
            dep,
            [o[4] for o in outs],
            [g for both_cores in gathered for g in both_cores],
            [o[2] for o in outs],
            [o[3] for o in outs],
            [o[5] for o in outs],
        )

    saved0 = attend(wqkv, x_cut, wo_all)
    sels = [tuple(selected(p) for p in both_cores) for both_cores in gather_pairs(after(named, saved0["qkv"]))]
    pairs = range(len(sels))
    far = gather_far(saved0["block"])
    saved0["rows"] = [pair(far[0])]
    outs0 = [experts(saved0["middle"], 0, saved0)]
    for j in pairs[1:]:
        saved0["rows"].append(pair(after(far[j], outs0[0][0])))
        outs0.append(experts(outs0[j - 1][0], j, saved0))
    dep = outs0[-1][0]
    terms, sent = reduce_pairs(outs0)
    shard0 = finish(saved0, split_sum(dep, terms, n_t, micro_count))
    gathered1 = gather_pairs(joined(pieces_tensor(after(cot, saved0["qkv"]))))
    saved1 = attend(dep, pieces_tensor(shifted(shard0, 1)), wo_all)
    far = gather_far(saved1["block"])
    saved1["rows"] = [pair(far[0])]
    back_outs1 = [experts_back(saved1["middle"], 0, saved1, gathered1)]
    for j in pairs[1:]:
        saved1["rows"].append(pair(after(far[j], back_outs1[0][0])))
        back_outs1.append(experts_back(back_outs1[j - 1][5], j, saved1, gathered1))
    terms, sent = reduce_pairs([o[:2] for o in back_outs1])
    experts1 = expert_grads(sent, gathered1, back_outs1)
    pieces = split_sum(experts1[0], terms, n_t, micro_count)
    outs1 = [experts(pieces[0], 0, saved1)]
    g_gain_m1, grad_middle1 = mid_back(saved1, cot, pieces, outs1[0][0])
    gm_shard = grad_middle1.astype(bf16)
    dep = gm_shard
    for j in pairs[1:]:
        outs1.append(experts(dep, j, saved1))
        dep = outs1[j][0]
    gqkv1, g_gain_a1, gm1, grad_in1 = attend_back(dep, saved1, grad_middle1, gm_shard)
    terms1, sent = reduce_pairs(outs1)
    returned = shifted(grad_in1, -1)
    far = gather_far(joined(pieces_tensor(returned)))
    gathered0 = [pair(far[0])]
    back_outs0 = [experts_back(gqkv1, 0, saved0, gathered0)]
    dep = back_outs0[0][5]
    for j in pairs[1:]:
        gathered0.append(pair(after(far[j], back_outs0[0][5])))
        back_outs0.append(experts_back(dep, j, saved0, gathered0))
        dep = back_outs0[j][5]
    pieces1 = split_sum(dep, terms1, n_t, micro_count)
    terms, sent = reduce_pairs([o[:2] for o in back_outs0])
    g_gate, g_up, g_down, g_router = lax.cond(
        first,
        lambda: tuple(expert_grads(after(sent, pieces1[0]), gathered0, back_outs0)),
        lambda: tuple(experts1),
    )
    pieces = split_sum(g_gate, terms, n_t, micro_count)
    shard1 = finish(saved1, pieces1, g_gate)
    g_gain_m0, grad_middle0 = mid_back(saved0, returned, pieces, pieces[0])
    gqkv0, g_gain_a0, gm0, grad_in0 = attend_back(
        dep, saved0, grad_middle0, grad_middle0.astype(bf16)
    )
    g_qkv, g_out = (
        jnp.where(first, a, b)
        for a, b in zip(
            shared_grads(saved0, gqkv0, gm0),
            shared_grads(saved1, gqkv1, gm1),
        )
    )
    g_gains = jnp.concatenate(
        [jnp.where(first, g_gain_a0, g_gain_a1), jnp.where(first, g_gain_m0, g_gain_m1)], axis=0
    )
    g_qkv = sum_expert(g_qkv.astype(bf16)).astype(f32)
    g_out = sum_expert(g_out.astype(bf16)).astype(f32)
    g_gains = sum_all_small(g_gains)
    g_router = jnp.roll(g_router[:, :NE], e_no * local_experts, axis=1)
    g_router = lax.psum(g_router, ("expert", "tensor"))

    def assemble(shard, *done):
        blocks = pieces_tensor(shard)
        if done:
            blocks[-1] = after(blocks[-1], *done)
        blocks = [p.reshape(micro_count, part, width) for p in blocks]
        whole = relative(jnp.concatenate(blocks, axis=1), 1, t_no, n_t)
        return whole[None]

    activations = assemble(after(jnp.where(first, shard0, shard1), gqkv0))
    input_grads = assemble(jnp.where(first, grad_in0, grad_in1))
    kv_width = key_projection.shape[2]
    return (
        activations,
        input_grads,
        g_gains[:1],
        g_qkv[None, :, :q_width],
        g_qkv[None, :, q_width : q_width + kv_width],
        g_qkv[None, :, q_width + kv_width :],
        g_out[None],
        g_gains[1:],
        g_router[None],
        g_gate[None],
        g_up[None],
        g_down[None],
    )


def solution(mesh):
    in_specs = (
        P(None, "expert", None),
        P(None, "expert", None),
        P(None, "expert"),
        P(None, "expert", None),
        P("section", None),
        P("section", None, "tensor"),
        P("section", None, "tensor"),
        P("section", None, "tensor"),
        P("section", "tensor", None),
        P("section", None),
        P("section", None, None),
        P("section", "expert", None, "tensor"),
        P("section", "expert", None, "tensor"),
        P("section", "expert", "tensor", None),
    )
    out_specs = (
        P("section", None, "expert", None),
        P("section", None, "expert", None),
        P("section", None),
        P("section", None, "tensor"),
        P("section", None, "tensor"),
        P("section", None, "tensor"),
        P("section", "tensor", None),
        P("section", None),
        P("section", None, None),
        P("section", "expert", None, "tensor"),
        P("section", "expert", None, "tensor"),
        P("section", "expert", "tensor", None),
    )
    return jax.shard_map(local, mesh=mesh, in_specs=in_specs, out_specs=out_specs, check_vma=False)
```
